256 devices in a mesh: sec: 32 (over z_lo, y, core), sym: 8 (over x, z_hi).
Axes of the slice: x: 4, y: 4, z: 8 (z_hi: 2, z_lo: 4; z = z_hi * 4 + z_lo), core: 2. Of those that a mesh axis runs over, the one named last changes fastest.
Arguments:
- start_state: float32 [32, 64, 128, 128], P('sec', 'sym'), may hold values from -6 to 6
- left_env: bfloat16 [32, 24, 64, 128, 128], P('sec', None, 'sym'), may hold values from -0.5 to 0.5
- right_env: bfloat16 [32, 24, 64, 128, 128], P('sec', None, 'sym'), may hold values from -0.5 to 0.5
- joining: int32 [32, 24, 64], P('sec'), may hold values from 0 to 63, as said below
- kept: int32 [32, 64], P('sec', 'sym'), may hold values from 64 to 128
Outputs:
- state: float32 [32, 64, 128, 128], P('sec', 'sym')
- energy: float32 [32], P('sec')
The draws below stay inside these ranges and needn't reach their ends.
Inputs may be any that keep to these rules, and one draw needn't show every extreme that they name: For every section s and term w, joining[s, w, :] is a permutation of the 64 sectors.
All inputs are finite; a program needn't handle non-finite values.
Results may differ from the reference program's by a relative error of at most 0.017.
Values may be sent and summed in bfloat16 or wider, within the bound.
No kernel may reach another device: no remote copies, remote signals or barrier semaphores. Data moves between devices by JAX's collectives and lax.ppermute only.
A program may use at most 128 MiB of HBM per device.

```python
import jax
import jax.numpy as jnp
from jax import lax

B = 128
W = 24
Q_DEV = 8
ITERS = 4
SECTIONS = 32
NQ = 64
N_SYM = 8


def draw_joining(key, part):
    key = jax.random.fold_in(key, 11)
    keys = jax.random.split(key, SECTIONS * W)
    tables = jax.vmap(lambda sub: jax.random.permutation(sub, NQ))(keys)
    return tables.reshape(SECTIONS, W, NQ).astype(jnp.int32)


def with_ends(drawn, rng, least, largest):
    place = [jax.random.randint(jax.random.fold_in(rng, axis), (), 0, length) for axis, length in enumerate(drawn.shape)]
    widest = drawn.shape.index(max(drawn.shape))
    beside = place[:widest] + [(place[widest] + 1) % drawn.shape[widest]] + place[widest + 1:]
    return drawn.at[tuple(place)].set(least).at[tuple(beside)].set(largest)


def levels(stream_key, extent, pieces, smallest, high):
    factor_of, own = 1.0, jax.random.fold_in(stream_key, 6)
    for dim, blocks in pieces:
        steps = jnp.exp(jax.random.uniform(jax.random.fold_in(own, dim), (blocks,), jnp.float32, smallest / len(pieces), high / len(pieces)))
        factor_of = factor_of * jnp.repeat(steps, extent[dim] // blocks).reshape([-1 if axis == dim else 1 for axis in range(len(extent))])
    return factor_of


def bell_draw(key, shape, deviation, bound, cuts=(), held_as=jnp.bfloat16):
    loudness = levels(key, shape, cuts, -0.22, 0.18) if cuts else 1.0
    array = jax.random.normal(key, shape, jnp.float32) * deviation * loudness
    return jnp.minimum(jnp.maximum(array, -bound), bound).astype(held_as)


def setup_inputs(seed: int = 0) -> dict:
    streams_of = jax.random.split(jax.random.key(seed), 6)
    start_state = bell_draw(streams_of[0], (SECTIONS, NQ, B, B), 1.0, 6.0, ((0, 32), (1, 8)), jnp.float32)
    left_env = bell_draw(streams_of[1], (SECTIONS, W, NQ, B, B), B ** -0.5, 0.5, ((0, 32), (2, 8)))
    right_env = bell_draw(streams_of[2], (SECTIONS, W, NQ, B, B), B ** -0.5, 0.5, ((0, 32), (2, 8)))
    joining = draw_joining(jax.random.fold_in(streams_of[5], 71), 0)
    kept = with_ends(jax.random.randint(streams_of[4], (SECTIONS, NQ), B // 2, B + 1), jax.random.fold_in(streams_of[4], 1), B // 2, B).astype(jnp.int32)
    return dict(start_state=start_state, left_env=left_env, right_env=right_env, joining=joining, kept=kept)


def apply_terms(left, right, state_b, table):

    def one_term(total, term_index):
        lw = left[term_index].astype(jnp.float32)
        rw = right[term_index].astype(jnp.float32)
        middle = jnp.einsum('qab,qbc->qac', lw, state_b.astype(jnp.float32)).astype(jnp.bfloat16)
        term = jnp.einsum('qac,qdc->qad', middle.astype(jnp.float32), rw)
        return (total.at[table[term_index]].add(term), None)
    start = jnp.zeros((NQ, B, B), jnp.float32)
    total, unused = lax.scan(one_term, start, jnp.arange(W))
    return total

def one_section(inputs):
    start_state, left, right, table, kept_row = inputs
    rows = lax.broadcasted_iota(jnp.int32, (B, B), 0)
    cols = lax.broadcasted_iota(jnp.int32, (B, B), 1)
    limit = kept_row[:, None, None]
    mask = ((rows[None] < limit) & (cols[None] < limit)).astype(jnp.float32)
    state = start_state * mask
    energy = jnp.zeros((), jnp.float32)
    for step in range(ITERS):
        state_b = state.astype(jnp.bfloat16)
        image = jnp.zeros((NQ, B, B), jnp.float32)
        for group in range(N_SYM):
            low = group * Q_DEV
            partial_value = apply_terms(left[:, low:low + Q_DEV], right[:, low:low + Q_DEV], state_b[low:low + Q_DEV], table[:, low:low + Q_DEV])
            rounded = lax.optimization_barrier(partial_value.astype(jnp.bfloat16))
            image = image + rounded.astype(jnp.float32)
        image = image * mask
        first = jnp.sum(state * state)
        second = jnp.sum(state * image)
        energy = second / first
        moved = state - 0.15 * (image - energy * state)
        size = jnp.sum(moved * moved)
        state = moved / jnp.sqrt(size / float(NQ * B * B) + 1e-06)
    return (state, energy)

def reference(start_state, left_env, right_env, joining, kept):
    renv = jnp.concatenate([right_env[1:], right_env[-1:]], axis=0)
    state, energy = lax.map(one_section, (start_state, left_env, renv, joining, kept))
    return (state, energy)
```

```python
import functools

import jax
import jax.numpy as jnp
from jax import lax
from jax.experimental import pallas as pl
from jax.experimental.pallas import tpu as pltpu
from jax.sharding import PartitionSpec as P

ITERS = 4
STEP = 0.15
SCALE = 2.0**-8
TERMS_PER_STEP = 4
ALONG_X = 4
ALONG_Z = 2
HALVES = 2
NT = (((1,), (1,)), ((), ()))
F32 = jnp.float32
BF16 = jnp.bfloat16


def params():
    return pltpu.CompilerParams(vmem_limit_bytes=48 * 2**20)


def sector_mask(limit, block):
    rows = lax.broadcasted_iota(jnp.int32, (block, block), 0)
    cols = lax.broadcasted_iota(jnp.int32, (block, block), 1)
    return ((rows < limit) & (cols < limit)).astype(F32)


def apply_kernel(first, slot_ref, kept_ref, at_end_ref, *refs):
    inputs = 1 if first else 4
    sources, (left_ref, here_ref, came_ref), refs = refs[:inputs], refs[inputs : inputs + 3], refs[inputs + 3 :]
    pieces, (vector_ref, total, middle, state_b, right_buffer, arrived) = refs[:8], refs[8:]
    step, steps = pl.program_id(0), pl.num_programs(0)
    terms, sectors, block = left_ref.shape[0], left_ref.shape[1], left_ref.shape[2]
    half = sectors // HALVES
    now = step % 2

    def copy(source_ref, at, slot):
        source = source_ref.at[pl.ds(at * terms, terms)]
        return pltpu.make_async_copy(source, right_buffer.at[slot], arrived.at[slot])

    def fetch(at, slot):
        @pl.when(at_end_ref[0] == 1)
        def _():
            copy(here_ref, at, slot).start()

        @pl.when(at_end_ref[0] != 1)
        def _():
            copy(came_ref, at, slot).start()

    @pl.when(step == 0)
    def _():
        fetch(0, 0)

    @pl.when(step + 1 < steps)
    def _():
        fetch(step + 1, 1 - now)

    @pl.when(step == 0)
    def _():
        total[...] = jnp.zeros_like(total)
        for q in range(sectors):
            mask = sector_mask(kept_ref[q], block)
            if first:
                value = sources[0][q] * mask
            else:
                own, came = sources[q // half], sources[2 + q // half]
                value = (own[q % half] + came[q % half].astype(F32)) * (mask * SCALE)
            vector_ref[q] = value
            state_b[q] = value.astype(BF16)

    for q in range(sectors):
        product = jnp.dot(
            left_ref[:, q].reshape(terms * block, block), state_b[q], preferred_element_type=F32
        )
        middle[:, q] = product.astype(BF16).reshape(terms, block, block)

    copy(here_ref, step, now).wait()
    right_ref = right_buffer.at[now]

    def one_term(k, carry):
        for q in range(sectors):
            term = lax.dot_general(middle[k, q], right_ref[k, q], NT, preferred_element_type=F32)
            slot = slot_ref[step * terms + k, q]
            total[slot] = total[slot] + term
        return carry

    lax.fori_loop(0, terms, one_term, 0)

    @pl.when(step == steps - 1)
    def _():
        per = ALONG_Z * half
        for index, piece in enumerate(pieces):
            for z in range(ALONG_Z):
                low = index * per + z * half
                piece[z] = total[low : low + half].astype(BF16)


def apply_operator(first, slots, kept, at_end, sources, left, rights):
    terms, sectors, block = left.shape[0], left.shape[1], left.shape[2]
    half = sectors // HALVES
    per = TERMS_PER_STEP
    whole = lambda shape: pl.BlockSpec(shape, lambda i, *_: (0,) * len(shape))
    stream = pl.BlockSpec((per, sectors, block, block), lambda i, *_: (i, 0, 0, 0))
    piece = (ALONG_Z, half, block, block)
    count = ALONG_X * HALVES
    out = pl.pallas_call(
        functools.partial(apply_kernel, first),
        grid_spec=pltpu.PrefetchScalarGridSpec(
            num_scalar_prefetch=3,
            grid=(terms // per,),
            in_specs=[whole(s.shape) for s in sources] + [stream] + [pl.BlockSpec(memory_space=pl.ANY)] * 2,
            out_specs=[whole(piece)] * count + [whole((sectors, block, block))],
            scratch_shapes=[
                pltpu.VMEM((count * ALONG_Z * half, block, block), F32),
                pltpu.VMEM((per, sectors, block, block), BF16),
                pltpu.VMEM((sectors, block, block), BF16),
                pltpu.VMEM((2, per, sectors, block, block), BF16),
                pltpu.SemaphoreType.DMA((2,)),
            ],
        ),
        out_shape=[jax.ShapeDtypeStruct(piece, BF16)] * count
        + [jax.ShapeDtypeStruct((sectors, block, block), F32)],
        compiler_params=params(),
        cost_estimate=pl.CostEstimate(
            flops=4 * terms * sectors * block**3, bytes_accessed=4 * terms * sectors * block**2, transcendentals=0
        ),
    )(slots, kept, at_end, *sources, left, *rights)
    return out[:count], out[count]


def dots(vectors, rows):
    newest = vectors[-1]
    sums = []
    for other in vectors:
        sums.append(jnp.sum(jnp.sum(newest * other, axis=0), axis=0, keepdims=True))
    sums += [jnp.zeros_like(sums[0])] * (rows - len(sums))
    return jnp.concatenate(sums, axis=0)


def dots_kernel(*refs):
    refs[-1][...] = dots([ref[...] for ref in refs[:-1]], 8)


def row_dots(vectors):
    return pl.pallas_call(
        dots_kernel,
        out_shape=jax.ShapeDtypeStruct((8, vectors[0].shape[-1]), F32),
        compiler_params=params(),
    )(*vectors)


def last_kernel(kept_ref, *refs):
    own, came, earlier = refs[:2], refs[2:4], refs[4:-2]
    vector_ref, dots_ref = refs[-2:]
    sectors, block = vector_ref.shape[0], vector_ref.shape[1]
    half = sectors // HALVES
    for q in range(sectors):
        mask = sector_mask(kept_ref[q], block) * SCALE
        vector_ref[q] = (own[q // half][q % half] + came[q // half][q % half].astype(F32)) * mask
    dots_ref[...] = dots([ref[...] for ref in earlier] + [vector_ref[...]], 8)


def last_vector(kept, own, came, earlier):
    shape = earlier[0].shape
    count = 4 + len(earlier)
    return pl.pallas_call(
        last_kernel,
        in_specs=[pl.BlockSpec(memory_space=pltpu.SMEM)] + [pl.BlockSpec(memory_space=pltpu.VMEM)] * count,
        out_shape=[jax.ShapeDtypeStruct(shape, F32), jax.ShapeDtypeStruct((8, shape[-1]), F32)],
        compiler_params=params(),
    )(kept, *own, *came, *earlier)


def combine_kernel(elements, *refs):
    grams, vectors, (state_ref, energy_ref) = refs[:8], refs[8 : 8 + ITERS + 1], refs[-2:]
    level = [ref[...] for ref in grams]
    while len(level) > 1:
        level = [level[i] + level[i + 1] for i in range(0, len(level), 2)]
    sums = jnp.broadcast_to(jnp.sum(level[0], axis=1, keepdims=True), level[0].shape)
    gram = {}
    for k in range(ITERS + 1):
        for j in range(k + 1):
            gram[k, j] = gram[j, k] = sums[8 * k + j : 8 * k + j + 1]

    def inner(one, two):
        result = None
        for i, x in enumerate(one):
            for j, y in enumerate(two):
                if x is not None and y is not None:
                    part = (x * y) * gram[i, j]
                    result = part if result is None else result + part
        return result

    weights = [jnp.ones_like(gram[0, 0])]
    energy = None
    for _ in range(ITERS):
        image = [None] + [w * (1.0 / SCALE) for w in weights]
        energy = inner(weights, image) / inner(weights, weights)
        moved = []
        for w, b in zip(weights + [None], image):
            if b is None:
                moved.append(w + STEP * energy * w)
            elif w is None:
                moved.append(-STEP * b)
            else:
                moved.append(w - STEP * (b - energy * w))
        scale = 1.0 / jnp.sqrt(inner(moved, moved) / float(elements) + 1e-6)
        weights = [m * scale for m in moved]
    energy_ref[...] = jnp.broadcast_to(energy, energy_ref.shape)
    for q in range(state_ref.shape[0]):
        value = weights[0] * vectors[0][q]
        for w, vector in zip(weights[1:], vectors[1:]):
            value = value + w * vector[q]
        state_ref[q] = value


def combine(grams, vectors, elements):
    shape = vectors[0].shape
    return pl.pallas_call(
        functools.partial(combine_kernel, elements),
        out_shape=[jax.ShapeDtypeStruct(shape, F32), jax.ShapeDtypeStruct((8, shape[-1]), F32)],
        compiler_params=params(),
    )(*grams, *vectors)


def around_x(value, steps):
    count = ALONG_X * ALONG_Z
    return lax.ppermute(value, "sym", [(i, (i + steps * ALONG_Z) % count) for i in range(count)])


def across(value, bits):
    count = ALONG_X * ALONG_Z
    return lax.ppermute(value, "sym", [(i, i ^ bits) for i in range(count)])


def add(*parts):
    total = parts[0].astype(F32)
    for part in parts[1:]:
        total = total + part.astype(F32)
    return total


def reduce_scatter(pieces):
    (own0, own1), (next0, next1), (far0, far1), (prev0, prev1) = [
        (pieces[2 * r], pieces[2 * r + 1]) for r in range(ALONG_X)
    ]
    went_right = around_x(far0, 1)
    went_left = around_x(far1, -1)
    from_left1 = around_x(next1, 1)
    from_right0 = around_x(prev0, -1)
    from_left0 = around_x(add(next0, went_right).astype(BF16), 1)
    from_right1 = around_x(add(prev1, went_left).astype(BF16), -1)
    sums = [add(own0, from_left0, from_right0), add(own1, from_left1, from_right1)]
    came = [across(s[1].astype(BF16), 1) for s in sums]
    return [s[0] for s in sums], came


def shards(start_state, left_env, right_env, joining, kept):
    sectors, block = start_state.shape[1], start_state.shape[2]
    half = sectors // HALVES
    count = lax.axis_size("sec")
    sym_index = lax.axis_index("sym")
    me_x, me_z = sym_index // ALONG_Z, sym_index % ALONG_Z
    at_end = jnp.reshape(lax.axis_index("sec") == count - 1, (1,)).astype(jnp.int32)
    rights = (right_env[0], lax.ppermute(right_env, "sec", [(s, s - 1) for s in range(1, count)])[0])
    left = left_env[0]
    table = lax.dynamic_slice_in_dim(joining[0], sym_index * sectors, sectors, 1)
    device, place = table // sectors, table % sectors
    piece = ((device // ALONG_Z - me_x) % ALONG_X) * HALVES + place // half
    slots = (piece * ALONG_Z + (device % ALONG_Z - me_z) % ALONG_Z) * half + place % half
    limits = kept[0]

    sources = [start_state[0]]
    vectors, rows = [], []
    for step in range(ITERS):
        pieces, vector = apply_operator(step == 0, slots, limits, at_end, sources, left, rights)
        vectors.append(vector)
        rows.append(row_dots(vectors))
        own, came = reduce_scatter(pieces)
        sources = own + came
    vector, last_rows = last_vector(limits, own, came, vectors)
    gram = jnp.concatenate(rows + [last_rows], axis=0)
    grams = [gram] + [across(gram, bits) for bits in range(1, ALONG_X * ALONG_Z)]
    elements = sectors * ALONG_X * ALONG_Z * block * block
    state, energy = combine(grams, vectors + [vector], elements)
    return (state[None], energy[0, :1])


def solution(mesh):
    return jax.shard_map(
        shards,
        mesh=mesh,
        in_specs=(
            P("sec", "sym", None, None),
            P("sec", None, "sym", None, None),
            P("sec", None, "sym", None, None),
            P("sec", None, None),
            P("sec", "sym"),
        ),
        out_specs=(P("sec", "sym", None, None), P("sec")),
        check_vma=False,
    )
```

```python
import functools

import jax
import jax.numpy as jnp
from jax import lax
from jax.experimental import pallas as pl
from jax.experimental.pallas import tpu as pltpu
from jax.sharding import PartitionSpec as P

ITERS = 4
STEP = 0.15
SCALE = 2.0**-8
GROUP = 16
STRAIGHT = (10, 9)
ALONG_X = 4
ALONG_Y = 4
ALONG_Z = 2
HALVES = 2
NT = (((1,), (1,)), ((), ()))
F32 = jnp.float32
BF16 = jnp.bfloat16


def params(mebibytes=24):
    return pltpu.CompilerParams(vmem_limit_bytes=mebibytes * 2**20)


def sector_mask(limit, block):
    rows = lax.broadcasted_iota(jnp.int32, (block, block), 0)
    cols = lax.broadcasted_iota(jnp.int32, (block, block), 1)
    return ((rows < limit) & (cols < limit)).astype(F32)


def gather_kernel(where_ref, here_ref, *refs):
    parts, (right_ref, arrived) = refs[:-2], refs[-2:]
    at_end, is_odd = where_ref[0] == 1, where_ref[1] == 1
    straight, (beside, around) = parts[:-2], parts[-2:]
    low = 0
    for part in straight + (beside,):
        rows = pl.ds(low, part.shape[0])
        low += part.shape[0]

        @pl.when(at_end)
        def _(rows=rows):
            pltpu.make_async_copy(here_ref.at[rows], right_ref.at[rows], arrived).start()

        if part is not beside:

            @pl.when(jnp.logical_not(at_end))
            def _(rows=rows, part=part):
                pltpu.make_async_copy(part, right_ref.at[rows], arrived).start()

        else:

            @pl.when(jnp.logical_not(at_end) & is_odd)
            def _(rows=rows):
                pltpu.make_async_copy(around, right_ref.at[rows], arrived).start()

            @pl.when(jnp.logical_not(at_end) & jnp.logical_not(is_odd))
            def _(rows=rows):
                pltpu.make_async_copy(beside, right_ref.at[rows], arrived).start()

    pltpu.make_async_copy(here_ref, right_ref, arrived).wait()


def gather_right(where, here, parts):
    anywhere = pl.BlockSpec(memory_space=pl.ANY)
    return pl.pallas_call(
        gather_kernel,
        in_specs=[pl.BlockSpec(memory_space=pltpu.SMEM), pl.BlockSpec(memory_space=pltpu.HBM)]
        + [anywhere] * len(parts),
        out_specs=pl.BlockSpec(memory_space=pltpu.VMEM),
        out_shape=jax.ShapeDtypeStruct(here.shape, here.dtype),
        scratch_shapes=[pltpu.SemaphoreType.DMA],
        compiler_params=params(),
    )(where, here, *parts)


def cut_kernel(value_ref, *refs):
    parts, arrived = refs[:-1], refs[-1]
    low, copies = 0, []
    for part in parts:
        for at in range(0, part.shape[0], 2):
            here = pl.ds(at, min(2, part.shape[0] - at))
            there = pl.ds(low + at, here.size)
            copies.append(pltpu.make_async_copy(value_ref.at[there], part.at[here], arrived.at[len(copies)]))
        low += part.shape[0]
    for copy in copies:
        copy.start()
    for copy in copies:
        copy.wait()


def cut(value, lengths):
    return pl.pallas_call(
        cut_kernel,
        in_specs=[pl.BlockSpec(memory_space=pltpu.HBM)],
        out_specs=[pl.BlockSpec(memory_space=pltpu.VMEM)] * len(lengths),
        out_shape=[jax.ShapeDtypeStruct((n,) + value.shape[1:], value.dtype) for n in lengths],
        scratch_shapes=[pltpu.SemaphoreType.DMA((value.shape[0],))],
        compiler_params=params(59),
    )(value)


def next_section(value):
    count = lax.axis_size("sec")
    pairs = [(s, s - 1) for s in range(1, count)]
    *straight, rest = cut(value, STRAIGHT + (value.shape[0] - sum(STRAIGHT),))
    parts = [lax.ppermute(part, "sec", pairs) for part in straight]
    beside = lax.ppermute(rest, "sec", [(s, d) for s, d in pairs if s % 2 == 1])

    def after(s, steps):
        ring = 2 * ALONG_Y
        return s // ring * ring + (s + 2 * steps) % ring

    around = rest
    for steps in range(2):
        around = lax.ppermute(around, "sec", [(after(s, steps), after(s, steps + 1)) for s in range(2, count, 2)])
    around = lax.ppermute(around, "sec", [(after(s, 2), s - 1) for s in range(2, count, 2)])
    return parts + [beside, around]


def middle_kernel(first, kept_ref, *refs):
    sources, (left_ref, vector_ref, middle_ref, state_b) = refs[:-4], refs[-4:]
    terms, sectors, block = left_ref.shape[0], left_ref.shape[1], left_ref.shape[2]
    half = sectors // HALVES
    middle_ref[terms * sectors] = jnp.zeros((block, block), BF16)
    for q in range(sectors):
        mask = sector_mask(kept_ref[q], block)
        if first:
            value = sources[0][q] * mask
        else:
            value = (sources[0][q // half, q % half] + sources[1][q // half, q % half].astype(F32)) * (mask * SCALE)
        vector_ref[q] = value
        state_b[q] = value.astype(BF16)
    for q in range(sectors):
        product = jnp.dot(
            left_ref[:, q].reshape(terms * block, block), state_b[q], preferred_element_type=F32
        )
        for w in range(terms):
            middle_ref[w * sectors + q] = product[w * block : (w + 1) * block].astype(BF16)


def apply_left(first, kept, sources, left):
    terms, sectors, block = left.shape[0], left.shape[1], left.shape[2]
    in_vmem = pl.BlockSpec(memory_space=pltpu.VMEM)
    return pl.pallas_call(
        functools.partial(middle_kernel, first),
        in_specs=[pl.BlockSpec(memory_space=pltpu.SMEM)] + [in_vmem] * (len(sources) + 1),
        out_specs=[in_vmem] * 2,
        out_shape=[
            jax.ShapeDtypeStruct((sectors, block, block), F32),
            jax.ShapeDtypeStruct((terms * sectors + 1, block, block), BF16),
        ],
        scratch_shapes=[pltpu.VMEM((sectors, block, block), BF16)],
        compiler_params=params(),
        cost_estimate=pl.CostEstimate(
            flops=8 * terms * sectors * block**3, bytes_accessed=4 * terms * sectors * block**2, transcendentals=0
        ),
    )(kept, *sources, left)


def target_kernel(pairs_ref, middle_ref, right_ref, *refs):
    pieces, total = refs[:-1], refs[-1]
    sectors = right_ref.shape[1]
    last = right_ref.shape[0] * sectors - 1
    total[...] = jnp.zeros_like(total)

    def group(index, carry):
        for i in range(GROUP):
            at = index * GROUP + i
            one, two, slot = pairs_ref[0, at], pairs_ref[1, at], pairs_ref[2, at]
            left = jnp.concatenate([middle_ref[one], middle_ref[two]], axis=1)
            one, two = jnp.minimum(one, last), jnp.minimum(two, last)
            right = jnp.concatenate(
                [right_ref[one // sectors, one % sectors], right_ref[two // sectors, two % sectors]], axis=1
            )
            total[slot] += lax.dot_general(left, right, NT, preferred_element_type=F32)
        return carry

    lax.fori_loop(0, pairs_ref[3, 0], group, 0)
    start = 0
    for piece in pieces:
        for index in range(piece.shape[0]):
            piece[index] = total[start : start + piece.shape[1]].astype(BF16)
            start += piece.shape[1]


def sum_targets(pairs, middle, right, shapes, share):
    terms, sectors, block = right.shape[0], right.shape[1], right.shape[2]
    in_vmem = pl.BlockSpec(memory_space=pltpu.VMEM)
    slots = sum(shape[0] * shape[1] for shape in shapes)
    return pl.pallas_call(
        target_kernel,
        in_specs=[pl.BlockSpec(memory_space=pltpu.SMEM), in_vmem, in_vmem],
        out_specs=[in_vmem] * len(shapes),
        out_shape=[jax.ShapeDtypeStruct(shape, BF16) for shape in shapes],
        scratch_shapes=[pltpu.VMEM((slots, block, block), F32)],
        compiler_params=params(),
        cost_estimate=pl.CostEstimate(
            flops=int(share * 16 * terms * sectors * block**3), bytes_accessed=1 << 20, transcendentals=0
        ),
    )(pairs, middle, right)


def pair_up(slots, low, high):
    slots = slots.reshape(-1)
    count = slots.shape[0]
    inside = (slots >= low) & (slots < high)
    number = jnp.arange(count)
    same = slots[:, None] == slots[None, :]
    rank = jnp.sum(same & (number[None, :] < number[:, None]), axis=1)
    opens = inside & (rank % 2 == 0)
    before = opens[None, :] & ((slots[None, :] < slots[:, None]) | (same & (number[None, :] < number[:, None])))
    place = jnp.sum(before, axis=1)
    place = jnp.where(rank % 2 == 0, place, place - 1)
    length = -(-(count // 2 + (high - low)) // GROUP) * GROUP
    at = inside[None, :] & (place[None, :] == jnp.arange(length)[:, None])
    is_first, is_second = at & (rank[None, :] % 2 == 0), at & (rank[None, :] % 2 == 1)

    def pick(chosen, values, otherwise):
        return jnp.sum(jnp.where(chosen, values[None, :] - otherwise, 0), axis=1) + otherwise

    groups = jnp.broadcast_to((jnp.sum(opens) + GROUP - 1) // GROUP, (length,))
    rows = [pick(is_first, number, count), pick(is_second, number, count), pick(is_first, slots - low, 0), groups]
    return jnp.stack(rows).astype(jnp.int32)


def dots(vectors, rows):
    newest = vectors[-1]
    sums = []
    for other in vectors:
        sums.append(jnp.sum(jnp.sum(newest * other, axis=0), axis=0, keepdims=True))
    sums += [jnp.zeros_like(sums[0])] * (rows - len(sums))
    return jnp.concatenate(sums, axis=0)


def dots_kernel(*refs):
    refs[-1][...] = dots([ref[...] for ref in refs[:-1]], 8)


def row_dots(vectors):
    return pl.pallas_call(
        dots_kernel,
        out_shape=jax.ShapeDtypeStruct((8, vectors[0].shape[-1]), F32),
        compiler_params=params(),
    )(*vectors)


def last_kernel(kept_ref, *refs):
    own, came, earlier = refs[0], refs[1], refs[2:-2]
    vector_ref, dots_ref = refs[-2:]
    sectors, block = vector_ref.shape[0], vector_ref.shape[1]
    half = sectors // HALVES
    for q in range(sectors):
        mask = sector_mask(kept_ref[q], block) * SCALE
        vector_ref[q] = (own[q // half, q % half] + came[q // half, q % half].astype(F32)) * mask
    dots_ref[...] = dots([ref[...] for ref in earlier] + [vector_ref[...]], 8)


def last_vector(kept, own, came, earlier):
    shape = earlier[0].shape
    count = 2 + len(earlier)
    return pl.pallas_call(
        last_kernel,
        in_specs=[pl.BlockSpec(memory_space=pltpu.SMEM)] + [pl.BlockSpec(memory_space=pltpu.VMEM)] * count,
        out_shape=[jax.ShapeDtypeStruct(shape, F32), jax.ShapeDtypeStruct((8, shape[-1]), F32)],
        compiler_params=params(),
    )(kept, own, came, *earlier)


def combine_kernel(elements, *refs):
    gram_ref, vectors, (state_ref, energy_ref) = refs[0], refs[1:-2], refs[-2:]
    sums = jnp.broadcast_to(jnp.sum(gram_ref[...], axis=1, keepdims=True), gram_ref.shape)
    gram = {}
    for k in range(ITERS + 1):
        for j in range(k + 1):
            gram[k, j] = gram[j, k] = sums[8 * k + j : 8 * k + j + 1]

    def inner(one, two):
        result = None
        for i, x in enumerate(one):
            for j, y in enumerate(two):
                if x is not None and y is not None:
                    part = (x * y) * gram[i, j]
                    result = part if result is None else result + part
        return result

    weights = [jnp.ones_like(gram[0, 0])]
    energy = None
    for _ in range(ITERS):
        image = [None] + [w * (1.0 / SCALE) for w in weights]
        energy = inner(weights, image) / inner(weights, weights)
        moved = []
        for w, b in zip(weights + [None], image):
            if b is None:
                moved.append(w + STEP * energy * w)
            elif w is None:
                moved.append(-STEP * b)
            else:
                moved.append(w - STEP * (b - energy * w))
        scale = 1.0 / jnp.sqrt(inner(moved, moved) / float(elements) + 1e-6)
        weights = [m * scale for m in moved]
    energy_ref[...] = jnp.broadcast_to(energy, energy_ref.shape)
    for q in range(state_ref.shape[0]):
        value = weights[0] * vectors[0][q]
        for w, vector in zip(weights[1:], vectors[1:]):
            value = value + w * vector[q]
        state_ref[q] = value


def combine(gram, vectors, elements):
    shape = vectors[0].shape
    return pl.pallas_call(
        functools.partial(combine_kernel, elements),
        out_shape=[jax.ShapeDtypeStruct(shape, F32), jax.ShapeDtypeStruct((8, shape[-1]), F32)],
        compiler_params=params(),
    )(gram, *vectors)


def around_x(value, steps):
    count = ALONG_X * ALONG_Z
    return lax.ppermute(value, "sym", [(i, (i + steps * ALONG_Z) % count) for i in range(count)])


def across(value, bits):
    count = ALONG_X * ALONG_Z
    return lax.ppermute(value, "sym", [(i, i ^ bits) for i in range(count)])


def add(*parts):
    total = parts[0].astype(F32)
    for part in parts[1:]:
        total = total + part.astype(F32)
    return total


def reduce_scatter(far, rest):
    prev, own, following = rest
    went_right = around_x(far[0], 1)
    went_left = around_x(far[1], -1)
    from_left = around_x(following.at[0].set(add(following[0], went_right).astype(BF16)), 1)
    from_right = around_x(prev.at[1].set(add(prev[1], went_left).astype(BF16)), -1)
    sums = add(own, from_left, from_right)
    return sums[:, 0], across(sums[:, 1].astype(BF16), 1)


def shards(start_state, left_env, right_env, joining, kept):
    sectors, block = start_state.shape[1], start_state.shape[2]
    half = sectors // HALVES
    count = lax.axis_size("sec")
    sym_index = lax.axis_index("sym")
    me_x, me_z = sym_index // ALONG_Z, sym_index % ALONG_Z
    section = lax.axis_index("sec")
    where = jnp.stack([section == count - 1, section % 2 == 1]).astype(jnp.int32)
    parts = next_section(right_env[0])
    left = left_env[0]
    table = lax.dynamic_slice_in_dim(joining[0], sym_index * sectors, sectors, 1)
    device, place = table // sectors, table % sectors
    piece = ((device // ALONG_Z - me_x + 2) % ALONG_X) * HALVES + place // half
    slots = (piece * ALONG_Z + (device % ALONG_Z - me_z) % ALONG_Z) * half + place % half
    per = HALVES * ALONG_Z * half
    far_pairs, rest_pairs = pair_up(slots, 0, per), pair_up(slots, per, ALONG_X * per)
    limits = kept[0]

    far_shape = (ALONG_Z, half, block, block)
    rest_shape = (HALVES * ALONG_Z, half, block, block)
    sources = [start_state[0]]
    vectors, rows, right = [], [], None
    for step in range(ITERS):
        vector, middle = apply_left(step == 0, limits, sources, left)
        if right is None:
            right = gather_right(where, right_env[0], parts)
        far = sum_targets(far_pairs, middle, right, [far_shape] * HALVES, 0.25)
        rest = sum_targets(rest_pairs, middle, right, [rest_shape] * (ALONG_X - 1), 0.75)
        rest = [r.reshape((HALVES,) + far_shape) for r in rest]
        vectors.append(vector)
        rows.append(row_dots(vectors))
        sources = reduce_scatter(far, rest)
    vector, last_rows = last_vector(limits, *sources, vectors)
    gram = jnp.concatenate(rows + [last_rows], axis=0)
    gram = (gram + across(gram, 2)) + (across(gram, 4) + across(gram, 6))
    gram = gram + across(gram, 1)
    elements = sectors * ALONG_X * ALONG_Z * block * block
    state, energy = combine(gram, vectors + [vector], elements)
    return (state[None], energy[0, :1])


def solution(mesh):
    return jax.shard_map(
        shards,
        mesh=mesh,
        in_specs=(
            P("sec", "sym", None, None),
            P("sec", None, "sym", None, None),
            P("sec", None, "sym", None, None),
            P("sec", None, None),
            P("sec", "sym"),
        ),
        out_specs=(P("sec", "sym", None, None), P("sec")),
        check_vma=False,
    )
```

```python
import functools

import jax
import jax.numpy as jnp
from jax import lax
from jax.experimental import pallas as pl
from jax.experimental.pallas import tpu as pltpu
from jax.sharding import PartitionSpec as P

ITERS = 4
STEP = 0.15
SCALE = 2.0**-8
GROUP = 16
STRAIGHT = (2, 10, 8)
ALONG_X = 4
ALONG_Y = 4
ALONG_Z = 2
HALVES = 2
NT = (((1,), (1,)), ((), ()))
F32 = jnp.float32
BF16 = jnp.bfloat16


def params(mebibytes=24):
    return pltpu.CompilerParams(vmem_limit_bytes=mebibytes * 2**20)


def sector_mask(limit, block):
    rows = lax.broadcasted_iota(jnp.int32, (block, block), 0)
    cols = lax.broadcasted_iota(jnp.int32, (block, block), 1)
    return ((rows < limit) & (cols < limit)).astype(F32)


def gather_kernel(where_ref, here_ref, *refs):
    parts, (right_ref, arrived) = refs[:-2], refs[-2:]
    at_end, is_odd = where_ref[0] == 1, where_ref[1] == 1
    straight, (beside, around) = parts[:-2], parts[-2:]
    low = 0
    for part in straight + (beside,):
        rows = pl.ds(low, part.shape[0])
        low += part.shape[0]

        @pl.when(at_end)
        def _(rows=rows):
            pltpu.make_async_copy(here_ref.at[rows], right_ref.at[rows], arrived).start()

        if part is not beside:

            @pl.when(jnp.logical_not(at_end))
            def _(rows=rows, part=part):
                pltpu.make_async_copy(part, right_ref.at[rows], arrived).start()

        else:

            @pl.when(jnp.logical_not(at_end) & is_odd)
            def _(rows=rows):
                pltpu.make_async_copy(around, right_ref.at[rows], arrived).start()

            @pl.when(jnp.logical_not(at_end) & jnp.logical_not(is_odd))
            def _(rows=rows):
                pltpu.make_async_copy(beside, right_ref.at[rows], arrived).start()

    pltpu.make_async_copy(here_ref, right_ref, arrived).wait()


def gather_right(where, here, parts):
    anywhere = pl.BlockSpec(memory_space=pl.ANY)
    return pl.pallas_call(
        gather_kernel,
        in_specs=[pl.BlockSpec(memory_space=pltpu.SMEM), pl.BlockSpec(memory_space=pltpu.HBM)]
        + [anywhere] * len(parts),
        out_specs=pl.BlockSpec(memory_space=pltpu.VMEM),
        out_shape=jax.ShapeDtypeStruct(here.shape, here.dtype),
        scratch_shapes=[pltpu.SemaphoreType.DMA],
        compiler_params=params(),
    )(where, here, *parts)


def cut_kernel(low, value_ref, after_ref, part_ref, arrived):
    copy = pltpu.make_async_copy(value_ref.at[pl.ds(low, part_ref.shape[0])], part_ref, arrived)
    copy.start()
    copy.wait()


def cut(value, low, after):
    shape = (value.shape[0] - low,) + value.shape[1:]
    return pl.pallas_call(
        functools.partial(cut_kernel, low),
        in_specs=[pl.BlockSpec(memory_space=pltpu.HBM), pl.BlockSpec(memory_space=pl.ANY)],
        out_specs=pl.BlockSpec(memory_space=pltpu.VMEM),
        out_shape=jax.ShapeDtypeStruct(shape, value.dtype),
        scratch_shapes=[pltpu.SemaphoreType.DMA],
        compiler_params=params(59),
    )(value, after)


def next_section(value):
    count = lax.axis_size("sec")
    pairs = [(s, s - 1) for s in range(1, count)]
    low, parts = 0, []
    for length in STRAIGHT:
        parts.append(lax.ppermute(value[low : low + length], "sec", pairs))
        low += length
    rest = cut(value, low, parts[0])
    beside = lax.ppermute(rest, "sec", [(s, d) for s, d in pairs if s % 2 == 1])

    def after(s, steps):
        ring = 2 * ALONG_Y
        return s // ring * ring + (s + 2 * steps) % ring

    around = rest
    for steps in range(2):
        around = lax.ppermute(around, "sec", [(after(s, steps), after(s, steps + 1)) for s in range(2, count, 2)])
    around = lax.ppermute(around, "sec", [(after(s, 2), s - 1) for s in range(2, count, 2)])
    return parts + [beside, around]


def middle_kernel(first, kept_ref, *refs):
    sources, (left_ref, vector_ref, middle_ref, state_b) = refs[:-4], refs[-4:]
    terms, sectors, block = left_ref.shape[0], left_ref.shape[1], left_ref.shape[2]
    half = sectors // HALVES
    middle_ref[terms * sectors] = jnp.zeros((block, block), BF16)
    for q in range(sectors):
        mask = sector_mask(kept_ref[q], block)
        if first:
            value = sources[0][q] * mask
        else:
            value = (sources[0][q // half, q % half] + sources[1][q // half, q % half].astype(F32)) * (mask * SCALE)
        vector_ref[q] = value
        state_b[q] = value.astype(BF16)
    for q in range(sectors):
        product = jnp.dot(
            left_ref[:, q].reshape(terms * block, block), state_b[q], preferred_element_type=F32
        )
        for w in range(terms):
            middle_ref[w * sectors + q] = product[w * block : (w + 1) * block].astype(BF16)


def apply_left(first, kept, sources, left):
    terms, sectors, block = left.shape[0], left.shape[1], left.shape[2]
    in_vmem = pl.BlockSpec(memory_space=pltpu.VMEM)
    return pl.pallas_call(
        functools.partial(middle_kernel, first),
        in_specs=[pl.BlockSpec(memory_space=pltpu.SMEM)] + [in_vmem] * (len(sources) + 1),
        out_specs=[in_vmem] * 2,
        out_shape=[
            jax.ShapeDtypeStruct((sectors, block, block), F32),
            jax.ShapeDtypeStruct((terms * sectors + 1, block, block), BF16),
        ],
        scratch_shapes=[pltpu.VMEM((sectors, block, block), BF16)],
        compiler_params=params(),
        cost_estimate=pl.CostEstimate(
            flops=8 * terms * sectors * block**3, bytes_accessed=4 * terms * sectors * block**2, transcendentals=0
        ),
    )(kept, *sources, left)


def target_kernel(pairs_ref, middle_ref, right_ref, *refs):
    pieces, total = refs[:-1], refs[-1]
    sectors = right_ref.shape[1]
    last = right_ref.shape[0] * sectors - 1
    total[...] = jnp.zeros_like(total)

    def group(index, carry):
        for i in range(GROUP):
            at = index * GROUP + i
            one, two, slot = pairs_ref[0, at], pairs_ref[1, at], pairs_ref[2, at]
            left = jnp.concatenate([middle_ref[one], middle_ref[two]], axis=1)
            one, two = jnp.minimum(one, last), jnp.minimum(two, last)
            right = jnp.concatenate(
                [right_ref[one // sectors, one % sectors], right_ref[two // sectors, two % sectors]], axis=1
            )
            total[slot] += lax.dot_general(left, right, NT, preferred_element_type=F32)
        return carry

    lax.fori_loop(0, pairs_ref[3, 0], group, 0)
    start = 0
    for piece in pieces:
        for index in range(piece.shape[0]):
            piece[index] = total[start : start + piece.shape[1]].astype(BF16)
            start += piece.shape[1]


def sum_targets(pairs, middle, right, shapes, share):
    terms, sectors, block = right.shape[0], right.shape[1], right.shape[2]
    in_vmem = pl.BlockSpec(memory_space=pltpu.VMEM)
    slots = sum(shape[0] * shape[1] for shape in shapes)
    return pl.pallas_call(
        target_kernel,
        in_specs=[pl.BlockSpec(memory_space=pltpu.SMEM), in_vmem, in_vmem],
        out_specs=[in_vmem] * len(shapes),
        out_shape=[jax.ShapeDtypeStruct(shape, BF16) for shape in shapes],
        scratch_shapes=[pltpu.VMEM((slots, block, block), F32)],
        compiler_params=params(),
        cost_estimate=pl.CostEstimate(
            flops=int(share * 16 * terms * sectors * block**3), bytes_accessed=1 << 20, transcendentals=0
        ),
    )(pairs, middle, right)


def pair_up(slots, low, high):
    slots = slots.reshape(-1)
    count = slots.shape[0]
    inside = (slots >= low) & (slots < high)
    number = jnp.arange(count)
    same = slots[:, None] == slots[None, :]
    rank = jnp.sum(same & (number[None, :] < number[:, None]), axis=1)
    opens = inside & (rank % 2 == 0)
    before = opens[None, :] & ((slots[None, :] < slots[:, None]) | (same & (number[None, :] < number[:, None])))
    place = jnp.sum(before, axis=1)
    place = jnp.where(rank % 2 == 0, place, place - 1)
    length = -(-(count // 2 + (high - low)) // GROUP) * GROUP
    at = inside[None, :] & (place[None, :] == jnp.arange(length)[:, None])
    is_first, is_second = at & (rank[None, :] % 2 == 0), at & (rank[None, :] % 2 == 1)

    def pick(chosen, values, otherwise):
        return jnp.sum(jnp.where(chosen, values[None, :] - otherwise, 0), axis=1) + otherwise

    groups = jnp.broadcast_to((jnp.sum(opens) + GROUP - 1) // GROUP, (length,))
    rows = [pick(is_first, number, count), pick(is_second, number, count), pick(is_first, slots - low, 0), groups]
    return jnp.stack(rows).astype(jnp.int32)


def dots(vectors, rows):
    newest = vectors[-1]
    sums = []
    for other in vectors:
        sums.append(jnp.sum(jnp.sum(newest * other, axis=0), axis=0, keepdims=True))
    sums += [jnp.zeros_like(sums[0])] * (rows - len(sums))
    return jnp.concatenate(sums, axis=0)


def dots_kernel(*refs):
    refs[-1][...] = dots([ref[...] for ref in refs[:-1]], 8)


def row_dots(vectors):
    return pl.pallas_call(
        dots_kernel,
        out_shape=jax.ShapeDtypeStruct((8, vectors[0].shape[-1]), F32),
        compiler_params=params(),
    )(*vectors)


def last_kernel(kept_ref, *refs):
    own, came, earlier = refs[0], refs[1], refs[2:-2]
    vector_ref, dots_ref = refs[-2:]
    sectors, block = vector_ref.shape[0], vector_ref.shape[1]
    half = sectors // HALVES
    for q in range(sectors):
        mask = sector_mask(kept_ref[q], block) * SCALE
        vector_ref[q] = (own[q // half, q % half] + came[q // half, q % half].astype(F32)) * mask
    dots_ref[...] = dots([ref[...] for ref in earlier] + [vector_ref[...]], 8)


def last_vector(kept, own, came, earlier):
    shape = earlier[0].shape
    count = 2 + len(earlier)
    return pl.pallas_call(
        last_kernel,
        in_specs=[pl.BlockSpec(memory_space=pltpu.SMEM)] + [pl.BlockSpec(memory_space=pltpu.VMEM)] * count,
        out_shape=[jax.ShapeDtypeStruct(shape, F32), jax.ShapeDtypeStruct((8, shape[-1]), F32)],
        compiler_params=params(),
    )(kept, own, came, *earlier)


def combine_kernel(elements, *refs):
    gram_ref, vectors, (state_ref, energy_ref) = refs[0], refs[1:-2], refs[-2:]
    sums = jnp.broadcast_to(jnp.sum(gram_ref[...], axis=1, keepdims=True), gram_ref.shape)
    gram = {}
    for k in range(ITERS + 1):
        for j in range(k + 1):
            gram[k, j] = gram[j, k] = sums[8 * k + j : 8 * k + j + 1]

    def inner(one, two):
        result = None
        for i, x in enumerate(one):
            for j, y in enumerate(two):
                if x is not None and y is not None:
                    part = (x * y) * gram[i, j]
                    result = part if result is None else result + part
        return result

    weights = [jnp.ones_like(gram[0, 0])]
    energy = None
    for _ in range(ITERS):
        image = [None] + [w * (1.0 / SCALE) for w in weights]
        energy = inner(weights, image) / inner(weights, weights)
        moved = []
        for w, b in zip(weights + [None], image):
            if b is None:
                moved.append(w + STEP * energy * w)
            elif w is None:
                moved.append(-STEP * b)
            else:
                moved.append(w - STEP * (b - energy * w))
        scale = 1.0 / jnp.sqrt(inner(moved, moved) / float(elements) + 1e-6)
        weights = [m * scale for m in moved]
    energy_ref[...] = jnp.broadcast_to(energy, energy_ref.shape)
    for q in range(state_ref.shape[0]):
        value = weights[0] * vectors[0][q]
        for w, vector in zip(weights[1:], vectors[1:]):
            value = value + w * vector[q]
        state_ref[q] = value


def combine(gram, vectors, elements):
    shape = vectors[0].shape
    return pl.pallas_call(
        functools.partial(combine_kernel, elements),
        out_shape=[jax.ShapeDtypeStruct(shape, F32), jax.ShapeDtypeStruct((8, shape[-1]), F32)],
        compiler_params=params(),
    )(gram, *vectors)


def around_x(value, steps):
    count = ALONG_X * ALONG_Z
    return lax.ppermute(value, "sym", [(i, (i + steps * ALONG_Z) % count) for i in range(count)])


def across(value, bits):
    count = ALONG_X * ALONG_Z
    return lax.ppermute(value, "sym", [(i, i ^ bits) for i in range(count)])


def add(*parts):
    total = parts[0].astype(F32)
    for part in parts[1:]:
        total = total + part.astype(F32)
    return total


def reduce_scatter(far, rest):
    prev, own, following = rest
    went_right = around_x(far[0], 1)
    went_left = around_x(far[1], -1)
    from_left = around_x(following.at[0].set(add(following[0], went_right).astype(BF16)), 1)
    from_right = around_x(prev.at[1].set(add(prev[1], went_left).astype(BF16)), -1)
    sums = add(own, from_left, from_right)
    return sums[:, 0], across(sums[:, 1].astype(BF16), 1)


def shards(start_state, left_env, right_env, joining, kept):
    sectors, block = start_state.shape[1], start_state.shape[2]
    half = sectors // HALVES
    count = lax.axis_size("sec")
    sym_index = lax.axis_index("sym")
    me_x, me_z = sym_index // ALONG_Z, sym_index % ALONG_Z
    section = lax.axis_index("sec")
    where = jnp.stack([section == count - 1, section % 2 == 1]).astype(jnp.int32)
    left = left_env[0]
    table = lax.dynamic_slice_in_dim(joining[0], sym_index * sectors, sectors, 1)
    device, place = table // sectors, table % sectors
    piece = ((device // ALONG_Z - me_x + 2) % ALONG_X) * HALVES + place // half
    slots = (piece * ALONG_Z + (device % ALONG_Z - me_z) % ALONG_Z) * half + place % half
    per = HALVES * ALONG_Z * half
    far_pairs, rest_pairs = pair_up(slots, 0, per), pair_up(slots, per, ALONG_X * per)
    limits = kept[0]

    far_shape = (ALONG_Z, half, block, block)
    rest_shape = (HALVES * ALONG_Z, half, block, block)
    sources = [start_state[0]]
    vectors, rows, right = [], [], None
    for step in range(ITERS):
        vector, middle = apply_left(step == 0, limits, sources, left)
        if right is None:
            right = gather_right(where, right_env[0], next_section(right_env[0]))
        far = sum_targets(far_pairs, middle, right, [far_shape] * HALVES, 0.25)
        rest = sum_targets(rest_pairs, middle, right, [rest_shape] * (ALONG_X - 1), 0.75)
        rest = [r.reshape((HALVES,) + far_shape) for r in rest]
        vectors.append(vector)
        rows.append(row_dots(vectors))
        sources = reduce_scatter(far, rest)
    vector, last_rows = last_vector(limits, *sources, vectors)
    gram = jnp.concatenate(rows + [last_rows], axis=0)
    gram = (gram + across(gram, 2)) + (across(gram, 4) + across(gram, 6))
    gram = gram + across(gram, 1)
    elements = sectors * ALONG_X * ALONG_Z * block * block
    state, energy = combine(gram, vectors + [vector], elements)
    return (state[None], energy[0, :1])


def solution(mesh):
    return jax.shard_map(
        shards,
        mesh=mesh,
        in_specs=(
            P("sec", "sym", None, None),
            P("sec", None, "sym", None, None),
            P("sec", None, "sym", None, None),
            P("sec", None, None),
            P("sec", "sym"),
        ),
        out_specs=(P("sec", "sym", None, None), P("sec")),
        check_vma=False,
    )
```

```python
import functools

import jax
import jax.numpy as jnp
from jax import lax
from jax.experimental import pallas as pl
from jax.experimental.pallas import tpu as pltpu
from jax.sharding import PartitionSpec as P

ITERS = 4
STEP = 0.15
SCALE = 2.0**-8
GROUP = 16
STRAIGHT = (3, 10, 7)
ALONG_X = 4
ALONG_Y = 4
ALONG_Z = 2
HALVES = 2
NT = (((1,), (1,)), ((), ()))
F32 = jnp.float32
BF16 = jnp.bfloat16


def params(mebibytes=24):
    return pltpu.CompilerParams(vmem_limit_bytes=mebibytes * 2**20)


def sector_mask(limit, block):
    rows = lax.broadcasted_iota(jnp.int32, (block, block), 0)
    cols = lax.broadcasted_iota(jnp.int32, (block, block), 1)
    return ((rows < limit) & (cols < limit)).astype(F32)


def gather_kernel(where_ref, here_ref, *refs):
    parts, (right_ref, arrived) = refs[:-2], refs[-2:]
    at_end, is_odd = where_ref[0] == 1, where_ref[1] == 1
    straight, (beside, around) = parts[:-2], parts[-2:]
    low = 0
    for part in straight + (beside,):
        rows = pl.ds(low, part.shape[0])
        low += part.shape[0]

        @pl.when(at_end)
        def _(rows=rows):
            pltpu.make_async_copy(here_ref.at[rows], right_ref.at[rows], arrived).start()

        if part is not beside:

            @pl.when(jnp.logical_not(at_end))
            def _(rows=rows, part=part):
                pltpu.make_async_copy(part, right_ref.at[rows], arrived).start()

        else:

            @pl.when(jnp.logical_not(at_end) & is_odd)
            def _(rows=rows):
                pltpu.make_async_copy(around, right_ref.at[rows], arrived).start()

            @pl.when(jnp.logical_not(at_end) & jnp.logical_not(is_odd))
            def _(rows=rows):
                pltpu.make_async_copy(beside, right_ref.at[rows], arrived).start()

    pltpu.make_async_copy(here_ref, right_ref, arrived).wait()


def gather_right(where, here, parts):
    anywhere = pl.BlockSpec(memory_space=pl.ANY)
    return pl.pallas_call(
        gather_kernel,
        in_specs=[pl.BlockSpec(memory_space=pltpu.SMEM), pl.BlockSpec(memory_space=pltpu.HBM)]
        + [anywhere] * len(parts),
        out_specs=pl.BlockSpec(memory_space=pltpu.VMEM),
        out_shape=jax.ShapeDtypeStruct(here.shape, here.dtype),
        scratch_shapes=[pltpu.SemaphoreType.DMA],
        compiler_params=params(),
    )(where, here, *parts)


def cut_kernel(low, value_ref, after_ref, part_ref, arrived):
    copy = pltpu.make_async_copy(value_ref.at[pl.ds(low, part_ref.shape[0])], part_ref, arrived)
    copy.start()
    copy.wait()


def cut(value, low, after):
    shape = (value.shape[0] - low,) + value.shape[1:]
    return pl.pallas_call(
        functools.partial(cut_kernel, low),
        in_specs=[pl.BlockSpec(memory_space=pltpu.HBM), pl.BlockSpec(memory_space=pl.ANY)],
        out_specs=pl.BlockSpec(memory_space=pltpu.VMEM),
        out_shape=jax.ShapeDtypeStruct(shape, value.dtype),
        scratch_shapes=[pltpu.SemaphoreType.DMA],
        compiler_params=params(59),
    )(value, after)


def next_section(value):
    count = lax.axis_size("sec")
    pairs = [(s, s - 1) for s in range(1, count)]
    low, parts = 0, []
    for length in STRAIGHT:
        parts.append(lax.ppermute(value[low : low + length], "sec", pairs))
        low += length
    rest = cut(value, low, parts[0])
    beside = lax.ppermute(rest, "sec", [(s, d) for s, d in pairs if s % 2 == 1])

    def after(s, steps):
        ring = 2 * ALONG_Y
        return s // ring * ring + (s + 2 * steps) % ring

    around = rest
    for steps in range(2):
        around = lax.ppermute(around, "sec", [(after(s, steps), after(s, steps + 1)) for s in range(2, count, 2)])
    around = lax.ppermute(around, "sec", [(after(s, 2), s - 1) for s in range(2, count, 2)])
    return parts + [beside, around]


def middle_kernel(first, kept_ref, *refs):
    sources, (left_ref, vector_ref, middle_ref, state_b) = refs[:-4], refs[-4:]
    terms, sectors, block = left_ref.shape[0], left_ref.shape[1], left_ref.shape[2]
    half = sectors // HALVES
    middle_ref[terms * sectors] = jnp.zeros((block, block), BF16)
    for q in range(sectors):
        mask = sector_mask(kept_ref[q], block)
        if first:
            value = sources[0][q] * mask
        else:
            value = (sources[0][q // half, q % half] + sources[1][q // half, q % half].astype(F32)) * (mask * SCALE)
        vector_ref[q] = value
        state_b[q] = value.astype(BF16)
    for q in range(sectors):
        product = jnp.dot(
            left_ref[:, q].reshape(terms * block, block), state_b[q], preferred_element_type=F32
        )
        for w in range(terms):
            middle_ref[w * sectors + q] = product[w * block : (w + 1) * block].astype(BF16)


def apply_left(first, kept, sources, left):
    terms, sectors, block = left.shape[0], left.shape[1], left.shape[2]
    in_vmem = pl.BlockSpec(memory_space=pltpu.VMEM)
    return pl.pallas_call(
        functools.partial(middle_kernel, first),
        in_specs=[pl.BlockSpec(memory_space=pltpu.SMEM)] + [in_vmem] * (len(sources) + 1),
        out_specs=[in_vmem] * 2,
        out_shape=[
            jax.ShapeDtypeStruct((sectors, block, block), F32),
            jax.ShapeDtypeStruct((terms * sectors + 1, block, block), BF16),
        ],
        scratch_shapes=[pltpu.VMEM((sectors, block, block), BF16)],
        compiler_params=params(),
        cost_estimate=pl.CostEstimate(
            flops=8 * terms * sectors * block**3, bytes_accessed=4 * terms * sectors * block**2, transcendentals=0
        ),
    )(kept, *sources, left)


def target_kernel(pairs_ref, middle_ref, right_ref, *refs):
    pieces, total = refs[:-1], refs[-1]
    sectors = right_ref.shape[1]
    last = right_ref.shape[0] * sectors - 1
    total[...] = jnp.zeros_like(total)

    def group(index, carry):
        for i in range(GROUP):
            at = index * GROUP + i
            one, two, slot = pairs_ref[0, at], pairs_ref[1, at], pairs_ref[2, at]
            left = jnp.concatenate([middle_ref[one], middle_ref[two]], axis=1)
            one, two = jnp.minimum(one, last), jnp.minimum(two, last)
            right = jnp.concatenate(
                [right_ref[one // sectors, one % sectors], right_ref[two // sectors, two % sectors]], axis=1
            )
            total[slot] += lax.dot_general(left, right, NT, preferred_element_type=F32)
        return carry

    lax.fori_loop(0, pairs_ref[3, 0], group, 0)
    start = 0
    for piece in pieces:
        for index in range(piece.shape[0]):
            piece[index] = total[start : start + piece.shape[1]].astype(BF16)
            start += piece.shape[1]


def sum_targets(pairs, middle, right, shapes, share):
    terms, sectors, block = right.shape[0], right.shape[1], right.shape[2]
    in_vmem = pl.BlockSpec(memory_space=pltpu.VMEM)
    slots = sum(shape[0] * shape[1] for shape in shapes)
    return pl.pallas_call(
        target_kernel,
        in_specs=[pl.BlockSpec(memory_space=pltpu.SMEM), in_vmem, in_vmem],
        out_specs=[in_vmem] * len(shapes),
        out_shape=[jax.ShapeDtypeStruct(shape, BF16) for shape in shapes],
        scratch_shapes=[pltpu.VMEM((slots, block, block), F32)],
        compiler_params=params(),
        cost_estimate=pl.CostEstimate(
            flops=int(share * 16 * terms * sectors * block**3), bytes_accessed=1 << 20, transcendentals=0
        ),
    )(pairs, middle, right)


def pair_up(slots, low, high):
    slots = slots.reshape(-1)
    count = slots.shape[0]
    inside = (slots >= low) & (slots < high)
    number = jnp.arange(count)
    same = slots[:, None] == slots[None, :]
    rank = jnp.sum(same & (number[None, :] < number[:, None]), axis=1)
    opens = inside & (rank % 2 == 0)
    before = opens[None, :] & ((slots[None, :] < slots[:, None]) | (same & (number[None, :] < number[:, None])))
    place = jnp.sum(before, axis=1)
    place = jnp.where(rank % 2 == 0, place, place - 1)
    length = -(-(count // 2 + (high - low)) // GROUP) * GROUP
    at = inside[None, :] & (place[None, :] == jnp.arange(length)[:, None])
    is_first, is_second = at & (rank[None, :] % 2 == 0), at & (rank[None, :] % 2 == 1)

    def pick(chosen, values, otherwise):
        return jnp.sum(jnp.where(chosen, values[None, :] - otherwise, 0), axis=1) + otherwise

    groups = jnp.broadcast_to((jnp.sum(opens) + GROUP - 1) // GROUP, (length,))
    rows = [pick(is_first, number, count), pick(is_second, number, count), pick(is_first, slots - low, 0), groups]
    return jnp.stack(rows).astype(jnp.int32)


def dots(vectors, rows):
    newest = vectors[-1]
    sums = []
    for other in vectors:
        sums.append(jnp.sum(jnp.sum(newest * other, axis=0), axis=0, keepdims=True))
    sums += [jnp.zeros_like(sums[0])] * (rows - len(sums))
    return jnp.concatenate(sums, axis=0)


def dots_kernel(*refs):
    refs[-1][...] = dots([ref[...] for ref in refs[:-1]], 8)


def row_dots(vectors):
    return pl.pallas_call(
        dots_kernel,
        out_shape=jax.ShapeDtypeStruct((8, vectors[0].shape[-1]), F32),
        compiler_params=params(),
    )(*vectors)


def last_kernel(kept_ref, *refs):
    own, came, earlier = refs[0], refs[1], refs[2:-2]
    vector_ref, dots_ref = refs[-2:]
    sectors, block = vector_ref.shape[0], vector_ref.shape[1]
    half = sectors // HALVES
    for q in range(sectors):
        mask = sector_mask(kept_ref[q], block) * SCALE
        vector_ref[q] = (own[q // half, q % half] + came[q // half, q % half].astype(F32)) * mask
    dots_ref[...] = dots([ref[...] for ref in earlier] + [vector_ref[...]], 8)


def last_vector(kept, own, came, earlier):
    shape = earlier[0].shape
    count = 2 + len(earlier)
    return pl.pallas_call(
        last_kernel,
        in_specs=[pl.BlockSpec(memory_space=pltpu.SMEM)] + [pl.BlockSpec(memory_space=pltpu.VMEM)] * count,
        out_shape=[jax.ShapeDtypeStruct(shape, F32), jax.ShapeDtypeStruct((8, shape[-1]), F32)],
        compiler_params=params(),
    )(kept, own, came, *earlier)


def combine_kernel(elements, *refs):
    gram_ref, vectors, (state_ref, energy_ref) = refs[0], refs[1:-2], refs[-2:]
    sums = jnp.broadcast_to(jnp.sum(gram_ref[...], axis=1, keepdims=True), gram_ref.shape)
    gram = {}
    for k in range(ITERS + 1):
        for j in range(k + 1):
            gram[k, j] = gram[j, k] = sums[8 * k + j : 8 * k + j + 1]

    def inner(one, two):
        result = None
        for i, x in enumerate(one):
            for j, y in enumerate(two):
                if x is not None and y is not None:
                    part = (x * y) * gram[i, j]
                    result = part if result is None else result + part
        return result

    weights = [jnp.ones_like(gram[0, 0])]
    energy = None
    for _ in range(ITERS):
        image = [None] + [w * (1.0 / SCALE) for w in weights]
        energy = inner(weights, image) / inner(weights, weights)
        moved = []
        for w, b in zip(weights + [None], image):
            if b is None:
                moved.append(w + STEP * energy * w)
            elif w is None:
                moved.append(-STEP * b)
            else:
                moved.append(w - STEP * (b - energy * w))
        scale = 1.0 / jnp.sqrt(inner(moved, moved) / float(elements) + 1e-6)
        weights = [m * scale for m in moved]
    energy_ref[...] = jnp.broadcast_to(energy, energy_ref.shape)
    for q in range(state_ref.shape[0]):
        value = weights[0] * vectors[0][q]
        for w, vector in zip(weights[1:], vectors[1:]):
            value = value + w * vector[q]
        state_ref[q] = value


def combine(gram, vectors, elements):
    shape = vectors[0].shape
    return pl.pallas_call(
        functools.partial(combine_kernel, elements),
        out_shape=[jax.ShapeDtypeStruct(shape, F32), jax.ShapeDtypeStruct((8, shape[-1]), F32)],
        compiler_params=params(),
    )(gram, *vectors)


def around_x(value, steps):
    count = ALONG_X * ALONG_Z
    return lax.ppermute(value, "sym", [(i, (i + steps * ALONG_Z) % count) for i in range(count)])


def across(value, bits):
    count = ALONG_X * ALONG_Z
    return lax.ppermute(value, "sym", [(i, i ^ bits) for i in range(count)])


def add(*parts):
    total = parts[0].astype(F32)
    for part in parts[1:]:
        total = total + part.astype(F32)
    return total


def reduce_scatter(far, rest):
    prev, own, following = rest
    went_right = around_x(far[0], 1)
    went_left = around_x(far[1], -1)
    from_left = around_x(following.at[0].set(add(following[0], went_right).astype(BF16)), 1)
    from_right = around_x(prev.at[1].set(add(prev[1], went_left).astype(BF16)), -1)
    sums = add(own, from_left, from_right)
    return sums[:, 0], across(sums[:, 1].astype(BF16), 1)


def shards(start_state, left_env, right_env, joining, kept):
    sectors, block = start_state.shape[1], start_state.shape[2]
    half = sectors // HALVES
    count = lax.axis_size("sec")
    sym_index = lax.axis_index("sym")
    me_x, me_z = sym_index // ALONG_Z, sym_index % ALONG_Z
    section = lax.axis_index("sec")
    where = jnp.stack([section == count - 1, section % 2 == 1]).astype(jnp.int32)
    left = left_env[0]
    table = lax.dynamic_slice_in_dim(joining[0], sym_index * sectors, sectors, 1)
    device, place = table // sectors, table % sectors
    piece = ((device // ALONG_Z - me_x + 2) % ALONG_X) * HALVES + place // half
    slots = (piece * ALONG_Z + (device % ALONG_Z - me_z) % ALONG_Z) * half + place % half
    per = HALVES * ALONG_Z * half
    far_pairs, rest_pairs = pair_up(slots, 0, per), pair_up(slots, per, ALONG_X * per)
    limits = kept[0]

    far_shape = (ALONG_Z, half, block, block)
    rest_shape = (HALVES * ALONG_Z, half, block, block)
    sources = [start_state[0]]
    vectors, rows, right = [], [], None
    for step in range(ITERS):
        vector, middle = apply_left(step == 0, limits, sources, left)
        if right is None:
            right = gather_right(where, right_env[0], next_section(right_env[0]))
        far = sum_targets(far_pairs, middle, right, [far_shape] * HALVES, 0.25)
        rest = sum_targets(rest_pairs, middle, right, [rest_shape] * (ALONG_X - 1), 0.75)
        rest = [r.reshape((HALVES,) + far_shape) for r in rest]
        vectors.append(vector)
        rows.append(row_dots(vectors))
        sources = reduce_scatter(far, rest)
    vector, last_rows = last_vector(limits, *sources, vectors)
    gram = jnp.concatenate(rows + [last_rows], axis=0)
    gram = (gram + across(gram, 2)) + (across(gram, 4) + across(gram, 6))
    gram = gram + across(gram, 1)
    elements = sectors * ALONG_X * ALONG_Z * block * block
    state, energy = combine(gram, vectors + [vector], elements)
    return (state[None], energy[0, :1])


def solution(mesh):
    return jax.shard_map(
        shards,
        mesh=mesh,
        in_specs=(
            P("sec", "sym", None, None),
            P("sec", None, "sym", None, None),
            P("sec", None, "sym", None, None),
            P("sec", None, None),
            P("sec", "sym"),
        ),
        out_specs=(P("sec", "sym", None, None), P("sec")),
        check_vma=False,
    )
```

```python
import functools

import jax
import jax.numpy as jnp
from jax import lax
from jax.experimental import pallas as pl
from jax.experimental.pallas import tpu as pltpu
from jax.sharding import PartitionSpec as P

ITERS = 4
STEP = 0.15
SCALE = 2.0**-8
GROUP = 16
STRAIGHT = (2, 10, 8)
ALONG_X = 4
ALONG_Y = 4
ALONG_Z = 2
HALVES = 2
NT = (((1,), (1,)), ((), ()))
F32 = jnp.float32
BF16 = jnp.bfloat16


def params(mebibytes=24):
    return pltpu.CompilerParams(vmem_limit_bytes=mebibytes * 2**20)


def sector_mask(limit, block):
    rows = lax.broadcasted_iota(jnp.int32, (block, block), 0)
    cols = lax.broadcasted_iota(jnp.int32, (block, block), 1)
    return ((rows < limit) & (cols < limit)).astype(F32)


def gather_kernel(low, last, where_ref, here_ref, *refs):
    parts, (right_ref, arrived) = refs[: -3 if last else -2], refs[-2:]
    at_end, is_odd = where_ref[0] == 1, where_ref[1] == 1
    straight, (beside, around) = (parts[:-2], parts[-2:]) if last else (parts, (None, None))
    begin = low
    for part in straight + ((beside,) if last else ()):
        rows = pl.ds(low, part.shape[0])
        low += part.shape[0]

        @pl.when(at_end)
        def _(rows=rows):
            pltpu.make_async_copy(here_ref.at[rows], right_ref.at[rows], arrived).start()

        if part is not beside:

            @pl.when(jnp.logical_not(at_end))
            def _(rows=rows, part=part):
                pltpu.make_async_copy(part, right_ref.at[rows], arrived).start()

        else:

            @pl.when(jnp.logical_not(at_end) & is_odd)
            def _(rows=rows):
                pltpu.make_async_copy(around, right_ref.at[rows], arrived).start()

            @pl.when(jnp.logical_not(at_end) & jnp.logical_not(is_odd))
            def _(rows=rows):
                pltpu.make_async_copy(beside, right_ref.at[rows], arrived).start()

    rows = pl.ds(begin, low - begin)
    pltpu.make_async_copy(here_ref.at[rows], right_ref.at[rows], arrived).wait()


def gather_right(where, here, parts):
    anywhere = pl.BlockSpec(memory_space=pl.ANY)
    in_vmem = pl.BlockSpec(memory_space=pltpu.VMEM)

    def call(low, some, held):
        return pl.pallas_call(
            functools.partial(gather_kernel, low, bool(held)),
            in_specs=[pl.BlockSpec(memory_space=pltpu.SMEM), pl.BlockSpec(memory_space=pltpu.HBM)]
            + [anywhere] * len(some)
            + [in_vmem] * len(held),
            out_specs=in_vmem,
            out_shape=jax.ShapeDtypeStruct(here.shape, here.dtype),
            scratch_shapes=[pltpu.SemaphoreType.DMA],
            input_output_aliases={2 + len(some): 0} if held else {},
            compiler_params=params(),
        )(where, here, *some, *held)

    early = len(STRAIGHT) - 1
    return call(sum(STRAIGHT[:early]), parts[early:], [call(0, parts[:early], [])])


def cut_kernel(low, value_ref, after_ref, part_ref, arrived):
    copy = pltpu.make_async_copy(value_ref.at[pl.ds(low, part_ref.shape[0])], part_ref, arrived)
    copy.start()
    copy.wait()


def cut(value, low, after):
    shape = (value.shape[0] - low,) + value.shape[1:]
    return pl.pallas_call(
        functools.partial(cut_kernel, low),
        in_specs=[pl.BlockSpec(memory_space=pltpu.HBM), pl.BlockSpec(memory_space=pl.ANY)],
        out_specs=pl.BlockSpec(memory_space=pltpu.VMEM),
        out_shape=jax.ShapeDtypeStruct(shape, value.dtype),
        scratch_shapes=[pltpu.SemaphoreType.DMA],
        compiler_params=params(59),
    )(value, after)


def next_section(value):
    count = lax.axis_size("sec")
    pairs = [(s, s - 1) for s in range(1, count)]
    low, parts = 0, []
    for length in STRAIGHT:
        parts.append(lax.ppermute(value[low : low + length], "sec", pairs))
        low += length
    rest = cut(value, low, parts[0])
    beside = lax.ppermute(rest, "sec", [(s, d) for s, d in pairs if s % 2 == 1])

    def after(s, steps):
        ring = 2 * ALONG_Y
        return s // ring * ring + (s + 2 * steps) % ring

    around = rest
    for steps in range(2):
        around = lax.ppermute(around, "sec", [(after(s, steps), after(s, steps + 1)) for s in range(2, count, 2)])
    around = lax.ppermute(around, "sec", [(after(s, 2), s - 1) for s in range(2, count, 2)])
    return parts + [beside, around]


def middle_kernel(first, kept_ref, *refs):
    sources, (left_ref, vector_ref, middle_ref, state_b) = refs[:-4], refs[-4:]
    terms, sectors, block = left_ref.shape[0], left_ref.shape[1], left_ref.shape[2]
    half = sectors // HALVES
    middle_ref[terms * sectors] = jnp.zeros((block, block), BF16)
    for q in range(sectors):
        mask = sector_mask(kept_ref[q], block)
        if first:
            value = sources[0][q] * mask
        else:
            value = (sources[0][q // half, q % half] + sources[1][q // half, q % half].astype(F32)) * (mask * SCALE)
        vector_ref[q] = value
        state_b[q] = value.astype(BF16)
    for q in range(sectors):
        product = jnp.dot(
            left_ref[:, q].reshape(terms * block, block), state_b[q], preferred_element_type=F32
        )
        for w in range(terms):
            middle_ref[w * sectors + q] = product[w * block : (w + 1) * block].astype(BF16)


def apply_left(first, kept, sources, left):
    terms, sectors, block = left.shape[0], left.shape[1], left.shape[2]
    in_vmem = pl.BlockSpec(memory_space=pltpu.VMEM)
    return pl.pallas_call(
        functools.partial(middle_kernel, first),
        in_specs=[pl.BlockSpec(memory_space=pltpu.SMEM)] + [in_vmem] * (len(sources) + 1),
        out_specs=[in_vmem] * 2,
        out_shape=[
            jax.ShapeDtypeStruct((sectors, block, block), F32),
            jax.ShapeDtypeStruct((terms * sectors + 1, block, block), BF16),
        ],
        scratch_shapes=[pltpu.VMEM((sectors, block, block), BF16)],
        compiler_params=params(),
        cost_estimate=pl.CostEstimate(
            flops=8 * terms * sectors * block**3, bytes_accessed=4 * terms * sectors * block**2, transcendentals=0
        ),
    )(kept, *sources, left)


def target_kernel(pairs_ref, middle_ref, right_ref, *refs):
    pieces, total = refs[:-1], refs[-1]
    sectors = right_ref.shape[1]
    last = right_ref.shape[0] * sectors - 1
    total[...] = jnp.zeros_like(total)

    def group(index, carry):
        for i in range(GROUP):
            at = index * GROUP + i
            one, two, slot = pairs_ref[0, at], pairs_ref[1, at], pairs_ref[2, at]
            left = jnp.concatenate([middle_ref[one], middle_ref[two]], axis=1)
            one, two = jnp.minimum(one, last), jnp.minimum(two, last)
            right = jnp.concatenate(
                [right_ref[one // sectors, one % sectors], right_ref[two // sectors, two % sectors]], axis=1
            )
            total[slot] += lax.dot_general(left, right, NT, preferred_element_type=F32)
        return carry

    lax.fori_loop(0, pairs_ref[3, 0], group, 0)
    start = 0
    for piece in pieces:
        for index in range(piece.shape[0]):
            piece[index] = total[start : start + piece.shape[1]].astype(BF16)
            start += piece.shape[1]


def sum_targets(pairs, middle, right, shapes, share):
    terms, sectors, block = right.shape[0], right.shape[1], right.shape[2]
    in_vmem = pl.BlockSpec(memory_space=pltpu.VMEM)
    slots = sum(shape[0] * shape[1] for shape in shapes)
    return pl.pallas_call(
        target_kernel,
        in_specs=[pl.BlockSpec(memory_space=pltpu.SMEM), in_vmem, in_vmem],
        out_specs=[in_vmem] * len(shapes),
        out_shape=[jax.ShapeDtypeStruct(shape, BF16) for shape in shapes],
        scratch_shapes=[pltpu.VMEM((slots, block, block), F32)],
        compiler_params=params(),
        cost_estimate=pl.CostEstimate(
            flops=int(share * 16 * terms * sectors * block**3), bytes_accessed=1 << 20, transcendentals=0
        ),
    )(pairs, middle, right)


def pair_up(slots, low, high):
    slots = slots.reshape(-1)
    count = slots.shape[0]
    inside = (slots >= low) & (slots < high)
    number = jnp.arange(count)
    same = slots[:, None] == slots[None, :]
    rank = jnp.sum(same & (number[None, :] < number[:, None]), axis=1)
    opens = inside & (rank % 2 == 0)
    before = opens[None, :] & ((slots[None, :] < slots[:, None]) | (same & (number[None, :] < number[:, None])))
    place = jnp.sum(before, axis=1)
    place = jnp.where(rank % 2 == 0, place, place - 1)
    length = -(-(count // 2 + (high - low)) // GROUP) * GROUP
    at = inside[None, :] & (place[None, :] == jnp.arange(length)[:, None])
    is_first, is_second = at & (rank[None, :] % 2 == 0), at & (rank[None, :] % 2 == 1)

    def pick(chosen, values, otherwise):
        return jnp.sum(jnp.where(chosen, values[None, :] - otherwise, 0), axis=1) + otherwise

    groups = jnp.broadcast_to((jnp.sum(opens) + GROUP - 1) // GROUP, (length,))
    rows = [pick(is_first, number, count), pick(is_second, number, count), pick(is_first, slots - low, 0), groups]
    return jnp.stack(rows).astype(jnp.int32)


def dots(vectors, rows):
    newest = vectors[-1]
    sums = []
    for other in vectors:
        sums.append(jnp.sum(jnp.sum(newest * other, axis=0), axis=0, keepdims=True))
    sums += [jnp.zeros_like(sums[0])] * (rows - len(sums))
    return jnp.concatenate(sums, axis=0)


def dots_kernel(*refs):
    refs[-1][...] = dots([ref[...] for ref in refs[:-1]], 8)


def row_dots(vectors):
    return pl.pallas_call(
        dots_kernel,
        out_shape=jax.ShapeDtypeStruct((8, vectors[0].shape[-1]), F32),
        compiler_params=params(),
    )(*vectors)


def last_kernel(kept_ref, *refs):
    own, came, earlier = refs[0], refs[1], refs[2:-2]
    vector_ref, dots_ref = refs[-2:]
    sectors, block = vector_ref.shape[0], vector_ref.shape[1]
    half = sectors // HALVES
    for q in range(sectors):
        mask = sector_mask(kept_ref[q], block) * SCALE
        vector_ref[q] = (own[q // half, q % half] + came[q // half, q % half].astype(F32)) * mask
    dots_ref[...] = dots([ref[...] for ref in earlier] + [vector_ref[...]], 8)


def last_vector(kept, own, came, earlier):
    shape = earlier[0].shape
    count = 2 + len(earlier)
    return pl.pallas_call(
        last_kernel,
        in_specs=[pl.BlockSpec(memory_space=pltpu.SMEM)] + [pl.BlockSpec(memory_space=pltpu.VMEM)] * count,
        out_shape=[jax.ShapeDtypeStruct(shape, F32), jax.ShapeDtypeStruct((8, shape[-1]), F32)],
        compiler_params=params(),
    )(kept, own, came, *earlier)


def combine_kernel(elements, *refs):
    gram_ref, vectors, (state_ref, energy_ref) = refs[0], refs[1:-2], refs[-2:]
    sums = jnp.broadcast_to(jnp.sum(gram_ref[...], axis=1, keepdims=True), gram_ref.shape)
    gram = {}
    for k in range(ITERS + 1):
        for j in range(k + 1):
            gram[k, j] = gram[j, k] = sums[8 * k + j : 8 * k + j + 1]

    def inner(one, two):
        result = None
        for i, x in enumerate(one):
            for j, y in enumerate(two):
                if x is not None and y is not None:
                    part = (x * y) * gram[i, j]
                    result = part if result is None else result + part
        return result

    weights = [jnp.ones_like(gram[0, 0])]
    energy = None
    for _ in range(ITERS):
        image = [None] + [w * (1.0 / SCALE) for w in weights]
        energy = inner(weights, image) / inner(weights, weights)
        moved = []
        for w, b in zip(weights + [None], image):
            if b is None:
                moved.append(w + STEP * energy * w)
            elif w is None:
                moved.append(-STEP * b)
            else:
                moved.append(w - STEP * (b - energy * w))
        scale = 1.0 / jnp.sqrt(inner(moved, moved) / float(elements) + 1e-6)
        weights = [m * scale for m in moved]
    energy_ref[...] = jnp.broadcast_to(energy, energy_ref.shape)
    for q in range(state_ref.shape[0]):
        value = weights[0] * vectors[0][q]
        for w, vector in zip(weights[1:], vectors[1:]):
            value = value + w * vector[q]
        state_ref[q] = value


def combine(gram, vectors, elements):
    shape = vectors[0].shape
    return pl.pallas_call(
        functools.partial(combine_kernel, elements),
        out_shape=[jax.ShapeDtypeStruct(shape, F32), jax.ShapeDtypeStruct((8, shape[-1]), F32)],
        compiler_params=params(),
    )(gram, *vectors)


def around_x(value, steps):
    count = ALONG_X * ALONG_Z
    return lax.ppermute(value, "sym", [(i, (i + steps * ALONG_Z) % count) for i in range(count)])


def across(value, bits):
    count = ALONG_X * ALONG_Z
    return lax.ppermute(value, "sym", [(i, i ^ bits) for i in range(count)])


def add(*parts):
    total = parts[0].astype(F32)
    for part in parts[1:]:
        total = total + part.astype(F32)
    return total


def reduce_scatter(far, rest):
    prev, own, following = rest
    went_right = around_x(far[0], 1)
    went_left = around_x(far[1], -1)
    from_left = around_x(following.at[0].set(add(following[0], went_right).astype(BF16)), 1)
    from_right = around_x(prev.at[1].set(add(prev[1], went_left).astype(BF16)), -1)
    sums = add(own, from_left, from_right)
    return sums[:, 0], across(sums[:, 1].astype(BF16), 1)


def shards(start_state, left_env, right_env, joining, kept):
    sectors, block = start_state.shape[1], start_state.shape[2]
    half = sectors // HALVES
    count = lax.axis_size("sec")
    sym_index = lax.axis_index("sym")
    me_x, me_z = sym_index // ALONG_Z, sym_index % ALONG_Z
    section = lax.axis_index("sec")
    where = jnp.stack([section == count - 1, section % 2 == 1]).astype(jnp.int32)
    left = left_env[0]
    table = lax.dynamic_slice_in_dim(joining[0], sym_index * sectors, sectors, 1)
    device, place = table // sectors, table % sectors
    piece = ((device // ALONG_Z - me_x + 2) % ALONG_X) * HALVES + place // half
    slots = (piece * ALONG_Z + (device % ALONG_Z - me_z) % ALONG_Z) * half + place % half
    per = HALVES * ALONG_Z * half
    far_pairs, rest_pairs = pair_up(slots, 0, per), pair_up(slots, per, ALONG_X * per)
    limits = kept[0]

    far_shape = (ALONG_Z, half, block, block)
    rest_shape = (HALVES * ALONG_Z, half, block, block)
    sources = [start_state[0]]
    vectors, rows, right = [], [], None
    for step in range(ITERS):
        vector, middle = apply_left(step == 0, limits, sources, left)
        if right is None:
            right = gather_right(where, right_env[0], next_section(right_env[0]))
        far = sum_targets(far_pairs, middle, right, [far_shape] * HALVES, 0.25)
        rest = sum_targets(rest_pairs, middle, right, [rest_shape] * (ALONG_X - 1), 0.75)
        rest = [r.reshape((HALVES,) + far_shape) for r in rest]
        vectors.append(vector)
        rows.append(row_dots(vectors))
        sources = reduce_scatter(far, rest)
    vector, last_rows = last_vector(limits, *sources, vectors)
    gram = jnp.concatenate(rows + [last_rows], axis=0)
    gram = (gram + across(gram, 2)) + (across(gram, 4) + across(gram, 6))
    gram = gram + across(gram, 1)
    elements = sectors * ALONG_X * ALONG_Z * block * block
    state, energy = combine(gram, vectors + [vector], elements)
    return (state[None], energy[0, :1])


def solution(mesh):
    return jax.shard_map(
        shards,
        mesh=mesh,
        in_specs=(
            P("sec", "sym", None, None),
            P("sec", None, "sym", None, None),
            P("sec", None, "sym", None, None),
            P("sec", None, None),
            P("sec", "sym"),
        ),
        out_specs=(P("sec", "sym", None, None), P("sec")),
        check_vma=False,
    )
```
